512 devices in a mesh: dp: 8 (over x, core), ctx: 64 (over z, y).
Axes of the slice: x: 4, y: 8, z: 8, core: 2. Of those that a mesh axis runs over, the one named last changes fastest.
Arguments:
- queries: bfloat16 [65536, 32, 128], P(('dp', 'ctx')), parts along dimension 0, may hold values from -10 to 10
- keys: bfloat16 [65536, 4, 128], P(('dp', 'ctx')), parts along dimension 0, may hold values from -10 to 10
- values: bfloat16 [65536, 4, 128], P(('dp', 'ctx')), parts along dimension 0, may hold values from -6 to 6
- segment: int32 [65536], P(('dp', 'ctx')), parts along dimension 0, may hold values from 0 to 31, never falling along the last dimension, each value on 1 to 768 neighbouring positions
- grad_out: bfloat16 [65536, 32, 128], P(('dp', 'ctx')), parts along dimension 0, may hold values from -6 to 6
Outputs:
- attended: bfloat16 [65536, 32, 128], P(('dp', 'ctx')), parts along dimension 0
- grad_queries: bfloat16 [65536, 32, 128], P(('dp', 'ctx')), parts along dimension 0
- grad_keys: bfloat16 [65536, 4, 128], P(('dp', 'ctx')), parts along dimension 0
- grad_values: bfloat16 [65536, 4, 128], P(('dp', 'ctx')), parts along dimension 0
The draws below stay inside these ranges and needn't reach their ends.
There are 8 independent parts, one for each index of `dp`. The reference program is written for one: setup_inputs(seed, part) draws one part's arguments, and reference() takes and returns one part's arrays. A program takes and returns all parts, laid end to end along the dimension named above; each array names one. Nothing has to cross between parts.
Inputs may be any that keep to these rules, and one draw needn't show every extreme that they name: `segment`: documents are runs of consecutive positions numbered in order; each holds 1 to 768 positions and one holds exactly 768.
All inputs are finite; a program needn't handle non-finite values.
Results may differ from the reference program's by a relative error of at most 0.012.
The reference program's roundings to bfloat16 on the way (of `probs_half` and `dscore`) count: a program that leaves them out, or rounds other values in their place, can miss the bound.
Values may be sent and summed in bfloat16 or wider, within the bound.
No kernel may reach another device: no remote copies, remote signals or barrier semaphores. Data moves between devices by JAX's collectives and lax.ppermute only.
A program may use at most 128 MiB of HBM per device.

```python
import math
import jax
import jax.numpy as jnp
import numpy as np
from jax import lax

HQ = 32
HK = 4
HD = 128
SEQ = 8192
MOST = 768
DOCS = 32


def draw_queries(key, part):
    key = jax.random.fold_in(key, 11)
    sample = jax.random.normal(key, (SEQ, HQ, HD), jnp.float32)
    return jnp.clip(sample, -10.0, 10.0).astype(jnp.bfloat16)


def draw_keys(key, part):
    key = jax.random.fold_in(key, 23)
    sample = jax.random.normal(key, (SEQ, HK, HD), jnp.float32)
    return jnp.clip(sample, -10.0, 10.0).astype(jnp.bfloat16)


def levels(stream_key, shape, split, least, largest):
    def one(dim, blocks):
        steps = jax.random.uniform(jax.random.fold_in(jax.random.fold_in(stream_key, 6), dim), (blocks,), jnp.float32, least / len(split), largest / len(split))
        return jnp.repeat(jnp.exp(steps), shape[dim] // blocks).reshape((-1,) + (1,) * (len(shape) - dim - 1))

    level = one(*split[0])
    for cut in split[1:]:
        level = level * one(*cut)
    return level


def profile(amount, total, bound, lean):
    loads = [(1 << 20) // math.isqrt(rank ** lean) + 1 for rank in range(2, amount + 1)]
    surplus, holding = total - bound - (amount - 1), [1] * (amount - 1)
    while surplus > 0:
        free = [i for i in range(amount - 1) if holding[i] < bound]
        whole, remaining = sum([loads[i] for i in free]), surplus
        for i in free:
            more = min(bound - holding[i], max(1, remaining * loads[i] // whole), surplus)
            holding[i] = holding[i] + more
            surplus = surplus - more
    return np.array([bound] + holding)


def uneven_parts(key, count, total, limit, lean):
    if count == 2:
        one = jax.random.randint(key, (), max(1, total - limit), min(limit, total - 1) + 1)
        return jnp.stack([one, total - one])
    lengths = jnp.asarray(profile(count, total, limit, lean), jnp.int32)
    couples = (count - 1) // 2
    source_of, receiver = lengths[1:1 + 2 * couples:2], lengths[2:2 + 2 * couples:2]
    room = jnp.minimum(source_of - 1, limit - receiver)
    shifted = jax.random.randint(jax.random.fold_in(key, 1), (couples,), 0, 1 << 20) % (room + 1)
    lengths = lengths.at[1:1 + 2 * couples:2].set(source_of - shifted).at[2:2 + 2 * couples:2].set(receiver + shifted)
    return lengths[jax.random.permutation(jax.random.fold_in(key, 2), count)]


def gaussian(stream_key, shape, scale, limit, cuts=(), held_as=jnp.bfloat16):
    values = scale * jax.random.normal(stream_key, shape, jnp.float32)
    if cuts:
        values = values * levels(stream_key, shape, cuts, -0.22, 0.18)
    return jnp.clip(values, -limit, limit).astype(held_as)


def setup_inputs(seed: int = 0, part: int = 0) -> dict:
    streams_of = jax.random.split(jax.random.key(seed), 6)
    part_splits = jax.random.split(jax.random.fold_in(streams_of[5], part), 6)
    return {
        "queries": draw_queries(jax.random.fold_in(jax.random.fold_in(streams_of[5], part), 71), part),
        "keys": draw_keys(jax.random.fold_in(jax.random.fold_in(streams_of[5], part), 71), part),
        "values": gaussian(part_splits[2], (SEQ, HK, HD), 1.0, 6.0, ((0, 64),)),
        "segment": jnp.searchsorted(jnp.cumsum(uneven_parts(part_splits[3], DOCS, SEQ, MOST, 2)), jnp.arange(SEQ), side="right").astype(jnp.int32),
        "grad_out": gaussian(part_splits[4], (SEQ, HQ, HD), 1.0, 6.0, ((0, 64),)),
    }


negative_fill = -1e30


def reference(queries, keys, values, segment, grad_out):
    length, head_count, head_dim = queries.shape
    group_count = keys.shape[1]
    per_group = head_count // group_count
    block_rows = min(512, length)
    block_count = length // block_rows
    window = block_rows + MOST
    softmax_scale = head_dim ** -0.5
    places = jnp.arange(length, dtype=jnp.int32)
    starts_here = jnp.concatenate([jnp.ones((1,), jnp.bool_), segment[1:] != segment[:-1]])
    doc_start = lax.cummax(jnp.where(starts_here, places, 0).astype(jnp.int32), axis=0)
    key_pad = jnp.concatenate([jnp.zeros((MOST, group_count, head_dim), keys.dtype), keys], 0)
    value_pad = jnp.concatenate([jnp.zeros((MOST, group_count, head_dim), values.dtype), values], 0)

    def one_block(running, number):
        key_total, value_total = running
        offset = (number * block_rows).astype(jnp.int32)
        query_block = lax.dynamic_slice_in_dim(queries, offset, block_rows, 0).astype(jnp.float32)
        query_block = query_block.reshape(block_rows, group_count, per_group, head_dim)
        grad_block = lax.dynamic_slice_in_dim(grad_out, offset, block_rows, 0).astype(jnp.float32)
        grad_block = grad_block.reshape(block_rows, group_count, per_group, head_dim)
        key_block = lax.dynamic_slice_in_dim(key_pad, offset, window, 0).astype(jnp.float32)
        value_block = lax.dynamic_slice_in_dim(value_pad, offset, window, 0).astype(jnp.float32)
        query_pos = offset + jnp.arange(block_rows, dtype=jnp.int32)
        key_pos = offset - MOST + jnp.arange(window, dtype=jnp.int32)
        block_start = lax.dynamic_slice_in_dim(doc_start, offset, block_rows, 0)
        visible = (key_pos[None, :] <= query_pos[:, None]) & (key_pos[None, :] >= block_start[:, None])
        scores = jnp.einsum('thgd,whd->htgw', query_block, key_block) * softmax_scale
        scores = jnp.where(visible[None, :, None, :], scores, negative_fill)
        row_max = jnp.max(scores, axis=-1, keepdims=True)
        shifted_exp = jnp.exp(scores - row_max)
        probs_full = shifted_exp / jnp.sum(shifted_exp, axis=-1, keepdims=True)
        probs_half = lax.optimization_barrier(probs_full.astype(jnp.bfloat16)).astype(jnp.float32)
        attended = jnp.einsum('htgw,whd->thgd', probs_half, value_block).astype(jnp.bfloat16)
        row_delta = jnp.sum(grad_block * attended.astype(jnp.float32), axis=-1)
        row_delta = jnp.transpose(row_delta, (1, 0, 2))
        dprobs = jnp.einsum('thgd,whd->htgw', grad_block, value_block)
        dscore = probs_full * (dprobs - row_delta[..., None])
        dscore = lax.optimization_barrier(dscore.astype(jnp.bfloat16)).astype(jnp.float32)
        grad_query = (jnp.einsum('htgw,whd->thgd', dscore, key_block) * softmax_scale).astype(jnp.bfloat16)
        grad_key = jnp.einsum('htgw,thgd->whd', dscore, query_block) * softmax_scale
        grad_value = jnp.einsum('htgw,thgd->whd', probs_half, grad_block)
        key_total = lax.dynamic_update_slice_in_dim(
            key_total, lax.dynamic_slice_in_dim(key_total, offset, window, 0) + grad_key, offset, 0)
        value_total = lax.dynamic_update_slice_in_dim(
            value_total, lax.dynamic_slice_in_dim(value_total, offset, window, 0) + grad_value, offset, 0)
        return (key_total, value_total), (attended, grad_query)

    initial = (jnp.zeros((length + MOST, group_count, head_dim), jnp.float32),
               jnp.zeros((length + MOST, group_count, head_dim), jnp.float32))
    totals, outputs = lax.scan(one_block, initial, jnp.arange(block_count, dtype=jnp.int32))
    attended = outputs[0].reshape(length, head_count, head_dim)
    grad_queries = outputs[1].reshape(length, head_count, head_dim)
    grad_keys = totals[0][MOST:].astype(jnp.bfloat16)
    grad_values = totals[1][MOST:].astype(jnp.bfloat16)
    return attended, grad_queries, grad_keys, grad_values
```

```python
import functools
import jax
import jax.numpy as jnp
from jax import lax
from jax.experimental import pallas as pl
from jax.experimental.pallas import tpu as pltpu
from jax.sharding import PartitionSpec as P
LOG2E = 1.4426950408889634
NB=7
ROWS=128; HD=128
NT=(((1,),(1,)),((),()))
TN=(((0,),(0,)),((),()))
NN=(((1,),(0,)),((),()))
def dot(a,b,d): return lax.dot_general(a,b,d,preferred_element_type=jnp.float32)

def kernel(q_ref, g_ref, own, b3, b6, u, v, att_ref, gq_ref, p0_ref, p3_ref, p6_ref, pu_ref, pv_ref,
           kw, vw, bias, pb, db, *, rc, scale):
    W=NB*ROWS
    n=8*ROWS+16
    def piece(k):
        return [(own,0),(u,0),(v,0),(b3,0),(u,n),(v,n),(b6,0)][k]
    hp=pl.program_id(0)
    @pl.when(hp==0)
    def _():
        segq=jnp.transpose(jnp.broadcast_to(own[8*ROWS:8*ROWS+1,:].astype(jnp.float32),(ROWS,ROWS)))
        for k in range(NB):
            r,o=piece(k)
            segk=jnp.broadcast_to(r[o+8*ROWS:o+8*ROWS+1,:].astype(jnp.float32),(ROWS,ROWS))
            vis=segk==segq
            if k==0:
                vis=vis & (lax.broadcasted_iota(jnp.int32,(ROWS,ROWS),1)<=lax.broadcasted_iota(jnp.int32,(ROWS,ROWS),0))
            bias[:, (6-k)*ROWS:(7-k)*ROWS]=jnp.where(vis,0.0,-1e30)
    for jj in range(2):
        for k in range(NB):
            r,o=piece(k)
            kw[(6-k)*ROWS:(7-k)*ROWS,:]=r[pl.ds(pl.multiple_of(o+(2*hp+jj)*ROWS,ROWS if o==0 else 16),ROWS),:]
            vw[(6-k)*ROWS:(7-k)*ROWS,:]=r[pl.ds(pl.multiple_of(o+(4+2*hp+jj)*ROWS,ROWS if o==0 else 16),ROWS),:]
        K=kw[...]; V=vw[...]
        tc=rc//8
        for c in range(8*ROWS//rc):
            ts=slice(c*tc,(c+1)*tc)
            qc=q_ref[ts,8*jj:8*jj+8,:].reshape(rc,HD)
            gc=g_ref[ts,8*jj:8*jj+8,:].reshape(rc,HD)
            s=dot(qc,K,NT).reshape(tc,8,W)*(scale*LOG2E)+bias[ts,:][:,None,:]
            s=s.reshape(rc,W)
            m=jnp.max(s,axis=-1,keepdims=True)
            e=jnp.exp2(s-m)
            l=jnp.sum(e,axis=-1,keepdims=True)
            p=e*(1.0/l)
            ph=p.astype(jnp.bfloat16)
            pb[c*rc:(c+1)*rc,:]=ph
            o=dot(ph,V,NN).astype(jnp.bfloat16)
            att_ref[ts,8*jj:8*jj+8,:]=o.reshape(tc,8,HD)
            delta=jnp.sum(gc.astype(jnp.float32)*o.astype(jnp.float32),axis=-1,keepdims=True)
            dp=dot(gc,V,NT)
            ds=(p*(dp-delta)).astype(jnp.bfloat16)
            db[c*rc:(c+1)*rc,:]=ds
            gq_ref[ts,8*jj:8*jj+8,:]=(dot(ds,K,NN)*scale).astype(jnp.bfloat16).reshape(tc,8,HD)
        Q=q_ref[:,8*jj:8*jj+8,:].reshape(8*ROWS,HD)
        G=g_ref[:,8*jj:8*jj+8,:].reshape(8*ROWS,HD)
        dk=dot(db[...],Q,TN)*scale
        dv=dot(pb[...],G,TN)
        for k in range(NB):
            dst,o=[(p0_ref,0),(pu_ref,0),(pv_ref,0),(p3_ref,0),(pu_ref,8*ROWS),(pv_ref,8*ROWS),(p6_ref,0)][k]
            sl=slice((6-k)*ROWS,(7-k)*ROWS)
            dst[pl.ds(pl.multiple_of(o+(2*hp+jj)*ROWS,ROWS),ROWS),:]=dk[sl].astype(dst.dtype)
            dst[pl.ds(pl.multiple_of(o+(4+2*hp+jj)*ROWS,ROWS),ROWS),:]=dv[sl].astype(dst.dtype)

def attn(q,g,own,b3,b6,u,v,rc=256):
    W=NB*ROWS
    hspec=pl.BlockSpec((ROWS,16,HD),lambda i:(0,i,0))
    full=lambda a: pl.BlockSpec(a.shape,lambda i:(0,)*len(a.shape))
    sd=jax.ShapeDtypeStruct
    outs=[sd(q.shape,jnp.bfloat16),sd(q.shape,jnp.bfloat16)]+[sd((8*ROWS,HD),jnp.float32)]*3+[sd((16*ROWS,HD),jnp.bfloat16)]*2
    return pl.pallas_call(functools.partial(kernel,rc=rc,scale=HD**-0.5),
        grid=(2,),
        in_specs=[hspec,hspec]+[full(x) for x in (own,b3,b6,u,v)],
        out_specs=[hspec,hspec]+[full(x) for x in outs[2:]],
        out_shape=outs,
        scratch_shapes=[pltpu.VMEM((W,HD),jnp.bfloat16),pltpu.VMEM((W,HD),jnp.bfloat16),pltpu.VMEM((ROWS,W),jnp.float32),
            pltpu.VMEM((8*ROWS,W),jnp.bfloat16),pltpu.VMEM((8*ROWS,W),jnp.bfloat16)],
        compiler_params=pltpu.CompilerParams(vmem_limit_bytes=48*2**20),
        name="attn",
    )(q,g,own,b3,b6,u,v)


def shift(value, steps):
    count = lax.axis_size("ctx")
    return lax.ppermute(value, "ctx", [(s, (s + steps) % count) for s in range(count)])


def shards(queries, keys, values, segment, grad_out):
    rows, groups, head = keys.shape
    n = 2 * groups * rows
    own = jnp.concatenate([
        jnp.transpose(keys, (1, 0, 2)).reshape(groups * rows, head),
        jnp.transpose(values, (1, 0, 2)).reshape(groups * rows, head),
        jnp.broadcast_to(segment.astype(jnp.bfloat16)[None, :], (16, rows)),
    ], 0)
    b3 = shift(own, 3)
    b6 = shift(own, 6)
    u = shift(jnp.concatenate([own, b3], 0), 1)
    v = shift(jnp.concatenate([b3, b6], 0), -1)
    att, gq, p0, p3, p6, pu, pv = attn(queries, grad_out, own, b3, b6, u, v)
    u = shift(pu, -1).astype(jnp.float32)
    v = shift(pv, 1).astype(jnp.float32)
    s3 = (p3 + u[n:] + v[:n]).astype(jnp.bfloat16)
    s6 = (p6 + v[n:]).astype(jnp.bfloat16)
    w = shift(s3, -3).astype(jnp.float32)
    z = shift(s6, -6).astype(jnp.float32)
    total = (p0 + u[:n] + w + z).astype(jnp.bfloat16).reshape(2, groups, rows, head)
    total = jnp.transpose(total, (0, 2, 1, 3))
    return att, gq, total[0], total[1]


def solution(mesh):
    part = P(("dp", "ctx"), None, None)
    return jax.shard_map(
        shards,
        mesh=mesh,
        in_specs=(part, part, part, P(("dp", "ctx")), part),
        out_specs=(part, part, part, part),
        check_vma=False,
    )
```
